512 devices in a mesh: blk: 32 (over y_hi, z), row: 16 (over x, y_lo, core).
Axes of the slice: x: 4, y: 4 (y_hi: 2, y_lo: 2; y = y_hi * 2 + y_lo), z: 16, core: 2. Of those that a mesh axis runs over, the one named last changes fastest.
Arguments:
- features: bfloat16 [65536, 128], P(('blk', 'row')), may hold values from -6 to 6
- targets: float32 [65536, 64], P(('blk', 'row')), may hold values from -6 to 6
- round_masks: int32 [2], replicated, may hold values from 1 to 31, as said below
Outputs:
- solution: float32 [65536, 64], P(('blk', 'row'))
- residual: float32 [65536, 64], P(('blk', 'row'))
The draws below stay inside these ranges and needn't reach their ends.
Inputs may be any that keep to these rules, and one draw needn't show every extreme that they name: `round_masks`: 2 distinct numbers, one of which is always 32 - 1.
All inputs are finite; a program needn't handle non-finite values.
Results may differ from the reference program's by a relative error of at most 0.0024.
The reference program's roundings to bfloat16 on the way count: a program that leaves them out, or rounds other values in their place, can miss the bound.
Values may be sent and summed in bfloat16 or wider, within the bound.
A program may use at most 64 MiB of HBM per device.

```python
import jax
import jax.numpy as jnp
from jax import lax

F = 128
TARGETS = 64
ROUNDS = 2
ITERS = 3
BLOCKS = 32
STREAMS = 65536
N_BLK = 32


def draw_round_masks(key, part):
    key = jax.random.fold_in(key, 29)
    order_key = jax.random.fold_in(key, 1)
    place_key = jax.random.fold_in(key, 2)
    others = jax.random.permutation(order_key, BLOCKS - 2) + 1
    chosen = jnp.concatenate([jnp.full((1,), BLOCKS - 1, jnp.int32), others[:ROUNDS - 1].astype(jnp.int32)])
    place = jax.random.randint(place_key, (), 0, ROUNDS, dtype=jnp.int32)
    return jnp.roll(chosen, place).astype(jnp.int32)


def block_scale(key, dims, shards, least, largest):
    gain, own = 1.0, jax.random.fold_in(key, 6)
    for position, parts in shards:
        steps = jnp.exp(jax.random.uniform(jax.random.fold_in(own, position), (parts,), jnp.float32, least / len(shards), largest / len(shards)))
        gain = gain * jnp.repeat(steps, dims[position] // parts).reshape([-1 if axis == position else 1 for axis in range(len(dims))])
    return gain


def noise(stream_key, shape, spread, reach, pieces=(), kind=jnp.bfloat16):
    drawn = jax.random.normal(stream_key, shape, jnp.float32) * spread
    if len(pieces) > 0:
        drawn = block_scale(stream_key, shape, pieces, -0.22, 0.18) * drawn
    return jnp.clip(drawn, min=-reach, max=reach).astype(kind)


def setup_inputs(seed: int = 0) -> dict:
    streams_of = jax.random.split(jax.random.key(seed), 4)
    return {
        "features": noise(streams_of[0], (STREAMS, F), 1.0, 6.0, ((0, 512),)),
        "targets": noise(streams_of[1], (STREAMS, TARGETS), 1.0, 6.0, ((0, 512),), jnp.float32),
        "round_masks": draw_round_masks(jax.random.fold_in(streams_of[3], 71), 0),
    }


RIDGE = 1.0


def kernel_tile(left, left_sq, right, right_sq):
    inner_products = lax.dot_general(left, right, (((1,), (1,)), ((), ())), preferred_element_type=jnp.float32)
    feature_width = left.shape[1]
    exponent = (2.0 * inner_products - left_sq[:, None] - right_sq[None, :]) / feature_width
    return jnp.exp(exponent).astype(jnp.bfloat16)


def reference(features, targets, round_masks):
    feature_width = features.shape[1]
    blocked = features.reshape(N_BLK, -1, feature_width)
    squares_all = jnp.sum(jnp.square(blocked.astype(jnp.float32)), axis=2)

    def operate(direction):
        rounded = direction.astype(jnp.bfloat16).reshape(N_BLK, -1, direction.shape[1])

        def one_block(block_index):
            own = blocked[block_index]
            own_sq = squares_all[block_index]
            accumulated = ROUNDS * jnp.dot(kernel_tile(own, own_sq, own, own_sq), rounded[block_index], preferred_element_type=jnp.float32)
            for round_index in range(ROUNDS):
                partner = jnp.bitwise_xor(block_index, round_masks[round_index]).astype(jnp.int32)
                tile = kernel_tile(own, own_sq, blocked[partner], squares_all[partner])
                accumulated = accumulated + jnp.dot(tile, rounded[partner], preferred_element_type=jnp.float32)
            return accumulated

        products = lax.map(one_block, jnp.arange(N_BLK, dtype=jnp.int32))
        return RIDGE * direction + products.reshape(direction.shape)

    solution = jnp.zeros(targets.shape, jnp.float32)
    residual = targets
    direction = targets
    norm_now = jnp.sum(residual * residual, axis=0)
    for iteration in range(ITERS):
        applied = operate(direction)
        step_size = norm_now / jnp.sum(direction * applied, axis=0)
        solution = solution + step_size * direction
        residual = residual - step_size * applied
        norm_next = jnp.sum(residual * residual, axis=0)
        direction = residual + (norm_next / norm_now) * direction
        norm_now = norm_next
    return solution, residual
```

```python
import functools

import jax
import jax.numpy as jnp
import numpy as np
from jax import lax
from jax.experimental import pallas as pl
from jax.experimental.pallas import tpu as pltpu
from jax.sharding import PartitionSpec as P

MESH = pl.DeviceIdType.MESH
ITERS = 3
BLOCKS = 32
LAST = BLOCKS - 1
NEAR, ACROSS = 1, 16
NX, NYL, NZ = 4, 2, 16
CHIPS = 3 * NX * NYL
COLS = 32
LANES = 128


def hops(a, b):
    dz = abs(a % NZ - b % NZ)
    return min(dz, NZ - dz) + 2 * (a // NZ != b // NZ)


def placement(mask):
    groups, seen = [], set()
    for b in range(BLOCKS):
        if b not in seen:
            group = [b, b ^ LAST, b ^ mask, b ^ LAST ^ mask]
            seen.update(group)
            groups.append(group)
    offsets = [0, NEAR, ACROSS, NEAR ^ ACROSS]

    def cost(group, base, twist):
        lengths = [hops(b, base ^ o ^ twist) for b, o in zip(group, offsets)]
        return max(lengths), sum(lengths)

    bases = [p for p in range(BLOCKS) if not p & (NEAR | ACROSS)]
    best = [[min((cost(g, base, t), t) for t in offsets) for base in bases] for g in groups]
    state = {0: ((0, 0), [])}
    for g in range(len(groups)):
        following = {}
        for used, ((longest, total), chosen) in state.items():
            for i in range(len(bases)):
                if used >> i & 1:
                    continue
                (top, plus), twist = best[g][i]
                value = (max(longest, top), total + plus)
                key = used | 1 << i
                if key not in following or value < following[key][0]:
                    following[key] = (value, chosen + [(i, twist)])
        state = following
    _, chosen = state[(1 << len(bases)) - 1]
    place = [0] * BLOCKS
    for group, (i, twist) in zip(groups, chosen):
        for b, o in zip(group, offsets):
            place[b] = bases[i] ^ o ^ twist
    return place


def two_sum(a, b):
    s = a + b
    bb = s - a
    return s, (a - (s - bb)) + (b - bb)


def renorm(s, e):
    h = s + e
    return h, e - (h - s)


def pair_add(a, b):
    s, e = two_sum(a[0], b[0])
    return renorm(s, e + (a[1] + b[1]))


def split(a):
    c = 4097.0 * a
    h = c - (c - a)
    return h, a - h


def two_prod(a, b):
    p = a * b
    ah, al = split(a)
    bh, bl = split(b)
    return p, ((ah * bh - p) + ah * bl + al * bh) + al * bl


def pair_mul(a, b):
    p, e = two_prod(a[0], b[0])
    return renorm(p, e + (a[0] * b[1] + a[1] * b[0]))


def pair_tree(pair):
    n = pair[0].shape[0]
    while n > 1:
        n //= 2
        pair = pair_add(tuple(v[:n] for v in pair), tuple(v[n:] for v in pair))
    return pair


def squares(block):
    wide = block.astype(jnp.float32)
    return jnp.sum(wide * wide, axis=1, keepdims=True)


def kernel(
    x_ref, t_ref, sol_ref, res_ref,
    feats, tile, q_buf, r_buf, d_buf, w_buf, sol_buf, part, plane, line, back, own_rows, own_sq,
    f_send, f_recv, g_send, g_recv, t_send, t_recv, c_sem, q_send, q_recv, p_send, p_recv, z_send, z_recv, b_sem,
):
    blk, row = lax.axis_index("blk"), lax.axis_index("row")
    yh, z = blk // NZ, blk % NZ
    x, yl, c = row // 4, (row // 2) % 2, row % 2
    chip = x * NYL + yl
    other = {"row": row - c + (1 - c)}
    me = chip

    def coset_peer(k):
        side, rel = k // 8, k % 8
        px, pyl = (x + rel // 2) % NX, (yl + rel) % NYL
        near = jnp.where(side == 1, 1, 0)
        across = jnp.where(side == 2, 1, 0)
        pz = z + near * (1 - 2 * (z % 2))
        pyh = (yh + across) % 2
        return (pyh * NZ + pz, px * 4 + pyl * 2 + c), side * 8 + px * NYL + pyl, side * 8 + chip

    def plane_peer(k):
        y = (yh * 2 + yl + k) % 4
        px = (x + k // 4) % NX
        return ((y // 2) * NZ + z, px * 4 + (y % 2) * 2 + c), px * 4 + y

    def line_peer(k):
        pz = (z + k) % NZ
        return (yh * NZ + pz, row), pz

    plane_me = x * 4 + yh * 2 + yl

    barrier = pltpu.get_barrier_semaphore()

    def greet(peer):
        pl.semaphore_signal(barrier, inc=1, device_id=peer, device_id_type=MESH)

    greet((blk, row - c + (1 - c)))
    for first, last, peer in ((8, CHIPS, coset_peer), (1, 16, plane_peer), (1, 16, line_peer)):
        lax.fori_loop(first, last, lambda k, _, peer=peer: greet(peer(k)[0]) or 0, 0)
    pl.semaphore_wait(barrier, 1 + (CHIPS - 8) + 15 + 15)

    def f_copy(k):
        peer, here, there = coset_peer(k)
        return pltpu.make_async_remote_copy(
            x_ref, feats.at[there, c], f_send.at[k], f_recv.at[there], device_id=peer, device_id_type=MESH)

    def f_arrival(slot):
        return pltpu.make_async_remote_copy(
            x_ref, feats.at[slot, c], f_send.at[0], f_recv.at[slot], device_id=(blk, row), device_id_type=MESH)

    def g_copy(slot):
        return pltpu.make_async_remote_copy(
            feats.at[slot, c], feats.at[slot, c], g_send.at[slot], g_recv.at[slot],
            device_id=(blk, row - c + (1 - c)), device_id_type=MESH)

    def g_arrival(slot):
        return pltpu.make_async_remote_copy(
            feats.at[slot, 1 - c], feats.at[slot, 1 - c], g_send.at[slot], g_recv.at[slot],
            device_id=(blk, row - c + (1 - c)), device_id_type=MESH)

    flipped = t_ref[...].T
    back[0] = flipped[:COLS]
    back[1] = flipped[COLS:]
    d_buf[me, c] = back[c]
    t_swap = pltpu.make_async_remote_copy(
        back.at[1 - c], d_buf.at[me, c], c_sem.at[0], c_sem.at[1],
        device_id=(blk, row - c + (1 - c)), device_id_type=MESH)
    t_swap.start()

    feats[me, c] = x_ref[...]
    g_copy(me).start()

    def send_features(k, _):
        f_copy(k).start()
        return 0

    lax.fori_loop(1, CHIPS, send_features, 0)
    pltpu.make_async_remote_copy(
        back.at[1 - c], d_buf.at[me, 1 - c], c_sem.at[0], c_sem.at[1],
        device_id=(blk, row - c + (1 - c)), device_id_type=MESH).wait_recv()

    def t_copy(k, slot):
        peer, here, there = coset_peer(k)
        return pltpu.make_async_remote_copy(
            d_buf.at[me], d_buf.at[there if slot is None else slot], t_send.at[k],
            t_recv.at[there if slot is None else slot], device_id=peer, device_id_type=MESH)

    def send_targets(k, _):
        t_copy(k, None).start()
        return 0

    lax.fori_loop(1, CHIPS, send_targets, 0)

    g_arrival(me).wait_recv()
    for half in range(2):
        block = feats[me, half]
        own_rows[half * LANES:(half + 1) * LANES] = block
        own_sq[:, half * LANES:(half + 1) * LANES] = jnp.broadcast_to(squares(block), (LANES, LANES)).T[0:8]

    def fill(slot, half):
        block = feats[slot, half]
        g = lax.dot_general(block, own_rows[...], (((1,), (1,)), ((), ())), preferred_element_type=jnp.float32)
        e = (2.0 * g - squares(block) - own_sq[0:1, :]) * (1.0 / 128.0)
        at = pl.multiple_of((slot * 2 + half) * LANES, LANES)
        tile[pl.ds(at, LANES), :] = jnp.exp(e).astype(jnp.bfloat16)

    fill(me, 0)
    fill(me, 1)

    def direct(k, _):
        _, slot, _ = coset_peer(k)
        f_arrival(slot).wait_recv()
        g_copy(slot).start()
        fill(slot, c)
        return 0

    lax.fori_loop(1, CHIPS, direct, 0)

    def forwarded(k, _):
        _, slot, _ = coset_peer(k)
        g_arrival(slot).wait_recv()
        fill(slot, 1 - c)
        return 0

    lax.fori_loop(1, CHIPS, forwarded, 0)

    def first(k, _):
        _, slot, _ = coset_peer(k)

        @pl.when(k > 0)
        def _():
            t_copy(k, slot).wait_recv()

        for half in range(2):
            v = d_buf[slot, half]
            r_buf[slot, half] = v
            at = pl.multiple_of((slot * 2 + half) * LANES, LANES)
            w_buf[:, pl.ds(at, LANES)] = v.astype(jnp.bfloat16)
        return 0

    lax.fori_loop(0, CHIPS, first, 0)

    def q_copy(it, k, slot):
        peer, here, there = coset_peer(k)
        at = there if slot is None else slot
        return pltpu.make_async_remote_copy(
            q_buf.at[it, me], q_buf.at[it, at], q_send.at[it, k], q_recv.at[it, at],
            device_id=peer, device_id_type=MESH)

    def p_copy(it, k, slot):
        peer, _ = plane_peer(k)
        at = plane_me if slot is None else slot
        return pltpu.make_async_remote_copy(
            part.at[it, 0], plane.at[it, at], p_send.at[it, k], p_recv.at[it, at],
            device_id=peer, device_id_type=MESH)

    def z_copy(it, k, slot):
        peer, _ = line_peer(k)
        at = z if slot is None else slot
        return pltpu.make_async_remote_copy(
            part.at[it, 1], line.at[it, at], z_send.at[it, k], z_recv.at[it, at],
            device_id=peer, device_id_type=MESH)

    def exchange(it, stage, gathered, mine, copy, peer, pair):
        msg = jnp.concatenate(pair, axis=0)
        part[it, stage] = msg
        gathered[it, mine] = msg

        def send(k, _):
            copy(it, k, None).start()
            return 0

        lax.fori_loop(1, 16, send, 0)

    def collect(it, gathered, copy, peer):
        def wait(k, _):
            copy(it, k, peer(k)[1]).wait_recv()
            return 0

        lax.fori_loop(1, 16, wait, 0)
        return pair_tree((gathered[it, :, 0, :], gathered[it, :, 1, :]))

    for it in range(ITERS):
        own = jnp.dot(w_buf[:, :16 * LANES], tile[:16 * LANES], preferred_element_type=jnp.float32)
        others = jnp.dot(w_buf[:, 16 * LANES:], tile[16 * LANES:], preferred_element_type=jnp.float32)
        products = 2.0 * own + others
        slot_q = min(it, 1)
        sums = None
        fresh = []
        for half in range(2):
            d, r = d_buf[me, half], r_buf[me, half]
            q = d + products[:, half * LANES:(half + 1) * LANES]
            fresh.append(q)
            pairs = [two_prod(d, q), two_prod(r, q), two_prod(q, q), two_prod(r, r)]
            pair = tuple(jnp.concatenate([p[i] for p in pairs], axis=0) for i in range(2))
            sums = pair if sums is None else pair_add(sums, pair)
        if it < ITERS - 1:
            for half in range(2):
                q_buf[it, me, half] = fresh[half]
        pair = pair_tree(tuple(v.T for v in sums))
        exchange(it, 0, plane, plane_me, p_copy, plane_peer, pair)
        if it < ITERS - 1:
            def send_q(k, _):
                q_copy(it, k, None).start()
                return 0

            lax.fori_loop(1, CHIPS, send_q, 0)
        pair = collect(it, plane, p_copy, plane_peer)
        exchange(it, 1, line, z, z_copy, line_peer, pair)
        total = collect(it, line, z_copy, line_peer)

        def entry(i):
            return tuple(v[:, i * COLS:(i + 1) * COLS] for v in total)

        dq, rq, qq, rr = (entry(i) for i in range(4))
        step = rr[0] / dq[0]
        if it < ITERS - 1:
            zero = jnp.zeros_like(step)
            minus = pair_mul((-2.0 * step, zero), rq)
            plus = pair_mul(two_prod(step, step), qq)
            new = pair_add(pair_add(rr, minus), plus)
            ratio = new[0] / rr[0]
        else:
            ratio = jnp.zeros_like(step)
        scalars = jnp.concatenate([step, ratio, step, ratio], axis=1)
        scalars = jnp.broadcast_to(scalars, (LANES, LANES)).T
        s, beta = scalars[:COLS], scalars[COLS:2 * COLS]

        for half in range(2):
            gain = s * d_buf[me, half]
            sol_buf[0, half] = gain if it == 0 else sol_buf[0, half] + gain

        if it < ITERS - 1:
            def update(k, _):
                _, slot, _ = coset_peer(k)

                @pl.when(k > 0)
                def _():
                    q_copy(it, k, slot).wait_recv()

                for half in range(2):
                    r = r_buf[slot, half] - s * q_buf[it, slot, half]
                    d = r + beta * d_buf[slot, half]
                    r_buf[slot, half] = r
                    d_buf[slot, half] = d
                    at = pl.multiple_of((slot * 2 + half) * LANES, LANES)
                    w_buf[:, pl.ds(at, LANES)] = d.astype(jnp.bfloat16)
                return 0

            if it == 0:
                def sent(k, _):
                    t_copy(k, None).wait_send()
                    return 0

                lax.fori_loop(1, CHIPS, sent, 0)
            lax.fori_loop(0, CHIPS, update, 0)
        else:
            for half in range(2):
                sol_buf[1, half] = r_buf[me, half] - s * fresh[half]

    for i in range(2):
        pltpu.make_async_remote_copy(
            sol_buf.at[i, 1 - c], own_back(back, i, c), b_sem.at[0, i], b_sem.at[1, i],
            device_id=(blk, row - c + (1 - c)), device_id_type=MESH).start()
    for i, out in ((0, sol_ref), (1, res_ref)):
        back[2 + 2 * i + c] = sol_buf[i, c]
        pltpu.make_async_remote_copy(
            sol_buf.at[i, 1 - c], own_back(back, i, 1 - c), b_sem.at[0, i], b_sem.at[1, i],
            device_id=(blk, row - c + (1 - c)), device_id_type=MESH).wait()
        out[...] = jnp.concatenate([back[2 + 2 * i], back[3 + 2 * i]], axis=0).T

    t_swap.wait_send()
    g_copy(me).wait_send()

    def drain(k, _):
        f_copy(k).wait_send()
        _, slot, _ = coset_peer(k)
        g_copy(slot).wait_send()
        for it in range(ITERS - 1):
            q_copy(it, k, None).wait_send()
        return 0

    lax.fori_loop(1, CHIPS, drain, 0)

    def drain_sums(k, _):
        for it in range(ITERS):
            p_copy(it, k, None).wait_send()
            z_copy(it, k, None).wait_send()
        return 0

    lax.fori_loop(1, 16, drain_sums, 0)


def own_back(back, i, core):
    return back.at[2 + 2 * i + core]


def conjugate_gradients(features, targets):
    f32, bf16 = jnp.float32, jnp.bfloat16
    dma = pltpu.SemaphoreType.DMA
    return pl.pallas_call(
        kernel,
        out_shape=[jax.ShapeDtypeStruct(targets.shape, f32)] * 2,
        in_specs=[pl.BlockSpec(memory_space=pltpu.VMEM)] * 2,
        out_specs=[pl.BlockSpec(memory_space=pltpu.VMEM)] * 2,
        scratch_shapes=[
            pltpu.VMEM((CHIPS, 2, LANES, LANES), bf16),
            pltpu.VMEM((CHIPS * 2 * LANES, 2 * LANES), bf16),
            pltpu.VMEM((2, CHIPS, 2, COLS, LANES), f32),
            pltpu.VMEM((CHIPS, 2, COLS, LANES), f32),
            pltpu.VMEM((CHIPS, 2, COLS, LANES), f32),
            pltpu.VMEM((COLS, CHIPS * 2 * LANES), bf16),
            pltpu.VMEM((2, 2, COLS, LANES), f32),
            pltpu.VMEM((ITERS, 2, 2, LANES), f32),
            pltpu.VMEM((ITERS, 16, 2, LANES), f32),
            pltpu.VMEM((ITERS, 16, 2, LANES), f32),
            pltpu.VMEM((6, COLS, LANES), f32),
            pltpu.VMEM((2 * LANES, LANES), bf16),
            pltpu.VMEM((8, 2 * LANES), f32),
            dma((CHIPS,)), dma((CHIPS,)), dma((CHIPS,)), dma((CHIPS,)), dma((CHIPS,)), dma((CHIPS,)), dma((2,)),
            dma((2, CHIPS)), dma((2, CHIPS)),
            dma((ITERS, 16)), dma((ITERS, 16)), dma((ITERS, 16)), dma((ITERS, 16)),
            dma((2, 2)),
        ],
        compiler_params=pltpu.CompilerParams(
            collective_id=0, has_side_effects=True, vmem_limit_bytes=40 * 1024 * 1024
        ),
    )(features, targets)


def local(features, targets, round_masks):
    plans = [placement(mask) for mask in range(1, LAST)]
    which = jnp.clip(round_masks[0] + round_masks[1] - LAST - 1, 0, LAST - 2)

    def mover(route):
        return lambda a, b: (lax.ppermute(a, "blk", route), lax.ppermute(b, "blk", route))

    there = [mover([(b, p) for b, p in enumerate(plan)]) for plan in plans]
    back = [mover([(p, b) for b, p in enumerate(plan)]) for plan in plans]
    features, targets = lax.switch(which, there, features, targets)
    solution, residual = conjugate_gradients(features, targets)
    return lax.switch(which, back, solution, residual)


def solution(mesh):
    in_specs = (P(("blk", "row"), None), P(("blk", "row"), None), P())
    out_specs = (P(("blk", "row"), None), P(("blk", "row"), None))
    return jax.shard_map(local, mesh=mesh, in_specs=in_specs, out_specs=out_specs, check_vma=False)
```

```python
import functools

import jax
import jax.numpy as jnp
import numpy as np
from jax import lax
from jax.experimental import pallas as pl
from jax.experimental.pallas import tpu as pltpu
from jax.sharding import PartitionSpec as P

MESH = pl.DeviceIdType.MESH
ITERS = 3
BLOCKS = 32
LAST = BLOCKS - 1
NEAR, ACROSS = 1, 16
NX, NYL, NZ = 4, 2, 16
CHIPS = 3 * NX * NYL
COLS = 32
LANES = 128


def hops(a, b):
    dz = abs(a % NZ - b % NZ)
    return min(dz, NZ - dz) + 2 * (a // NZ != b // NZ)


def placement(mask):
    groups, seen = [], set()
    for b in range(BLOCKS):
        if b not in seen:
            group = [b, b ^ LAST, b ^ mask, b ^ LAST ^ mask]
            seen.update(group)
            groups.append(group)
    offsets = [0, NEAR, ACROSS, NEAR ^ ACROSS]

    def cost(group, base, twist):
        lengths = [hops(b, base ^ o ^ twist) for b, o in zip(group, offsets)]
        return (max(lengths) if min(lengths) else BLOCKS), sum(lengths)

    bases = [p for p in range(BLOCKS) if not p & (NEAR | ACROSS)]
    best = [[min((cost(g, base, t), t) for t in offsets) for base in bases] for g in groups]
    state = {0: ((0, 0), [])}
    for g in range(len(groups)):
        following = {}
        for used, ((longest, total), chosen) in state.items():
            for i in range(len(bases)):
                if used >> i & 1:
                    continue
                (top, plus), twist = best[g][i]
                value = (max(longest, top), total + plus)
                key = used | 1 << i
                if key not in following or value < following[key][0]:
                    following[key] = (value, chosen + [(i, twist)])
        state = following
    _, chosen = state[(1 << len(bases)) - 1]
    place = [0] * BLOCKS
    for group, (i, twist) in zip(groups, chosen):
        for b, o in zip(group, offsets):
            place[b] = bases[i] ^ o ^ twist
    return place


def two_sum(a, b):
    s = a + b
    bb = s - a
    return s, (a - (s - bb)) + (b - bb)


def renorm(s, e):
    h = s + e
    return h, e - (h - s)


def pair_add(a, b):
    s, e = two_sum(a[0], b[0])
    return renorm(s, e + (a[1] + b[1]))


def split(a):
    c = 4097.0 * a
    h = c - (c - a)
    return h, a - h


def two_prod(a, b):
    p = a * b
    ah, al = split(a)
    bh, bl = split(b)
    return p, ((ah * bh - p) + ah * bl + al * bh) + al * bl


def pair_mul(a, b):
    p, e = two_prod(a[0], b[0])
    return renorm(p, e + (a[0] * b[1] + a[1] * b[0]))


def pair_tree(pair):
    n = pair[0].shape[0]
    while n > 1:
        n //= 2
        pair = pair_add(tuple(v[:n] for v in pair), tuple(v[n:] for v in pair))
    return pair


def squares(block):
    wide = block.astype(jnp.float32)
    return jnp.sum(wide * wide, axis=1, keepdims=True)


def looked_up(table, index):
    value = jnp.int32(table[0])
    for i in range(1, len(table)):
        value = jnp.where(index == i, table[i], value)
    return value


def kernel(
    x_ref, t_ref, out_ref,
    feats, tile, q_buf, r_buf, d_buf, w_buf, part, plane, line, own_rows, own_sq,
    f_send, f_recv, g_send, g_recv, t_send, t_recv, q_send, q_recv, p_send, p_recv, z_send, z_recv,
):
    blk, row = lax.axis_index("blk"), lax.axis_index("row")
    yh, z = blk // NZ, blk % NZ
    x, yl, c = row // 4, (row // 2) % 2, row % 2
    chip = x * NYL + yl
    me = chip

    def coset_peer(k):
        side, rel = k // 8, k % 8
        px, pyl = (x + rel // 2) % NX, (yl + rel) % NYL
        near = jnp.where(side == 1, 1, 0)
        across = jnp.where(side == 2, 1, 0)
        pz = z + near * (1 - 2 * (z % 2))
        pyh = (yh + across) % 2
        return (pyh * NZ + pz, px * 4 + pyl * 2 + c), side * 8 + px * NYL + pyl, side * 8 + chip

    def plane_peer(k):
        y = (yh * 2 + yl + k) % 4
        px = (x + k // 4) % NX
        return ((y // 2) * NZ + z, px * 4 + (y % 2) * 2 + c), px * 4 + y

    def line_peer(k):
        pz = (z + k) % NZ
        return (yh * NZ + pz, row), pz

    plane_me = x * 4 + yh * 2 + yl

    barrier = pltpu.get_barrier_semaphore()

    def greet(peer):
        pl.semaphore_signal(barrier, inc=1, device_id=peer, device_id_type=MESH)

    greet((blk, row - c + (1 - c)))
    for first, last, peer in ((8, CHIPS, coset_peer), (1, 16, plane_peer), (1, 16, line_peer)):
        lax.fori_loop(first, last, lambda k, _, peer=peer: greet(peer(k)[0]) or 0, 0)
    pl.semaphore_wait(barrier, 1 + (CHIPS - 8) + 15 + 15)

    def f_copy(k):
        peer, here, there = coset_peer(k)
        return pltpu.make_async_remote_copy(
            x_ref.at[c], feats.at[there, c], f_send.at[k], f_recv.at[there], device_id=peer, device_id_type=MESH)

    def f_arrival(slot):
        return pltpu.make_async_remote_copy(
            feats.at[slot, c], feats.at[slot, c], f_send.at[0], f_recv.at[slot], device_id=(blk, row), device_id_type=MESH)

    def g_copy(slot):
        return pltpu.make_async_remote_copy(
            feats.at[slot, c], feats.at[slot, c], g_send.at[slot], g_recv.at[slot],
            device_id=(blk, row - c + (1 - c)), device_id_type=MESH)

    def g_arrival(slot):
        return pltpu.make_async_remote_copy(
            feats.at[slot, 1 - c], feats.at[slot, 1 - c], g_send.at[slot], g_recv.at[slot],
            device_id=(blk, row - c + (1 - c)), device_id_type=MESH)

    def send_features(k, _):
        f_copy(k).start()
        return 0

    lax.fori_loop(1, CHIPS, send_features, 0)
    def t_copy(k, slot):
        peer, here, there = coset_peer(k)
        return pltpu.make_async_remote_copy(
            t_ref, d_buf.at[there if slot is None else slot], t_send.at[k],
            t_recv.at[there if slot is None else slot], device_id=peer, device_id_type=MESH)

    def send_targets(k, _):
        t_copy(k, None).start()
        return 0

    lax.fori_loop(1, CHIPS, send_targets, 0)

    d_buf[me] = t_ref[...]
    for half in range(2):
        block = x_ref[half]
        feats[me, half] = block
        own_rows[half * LANES:(half + 1) * LANES] = block
        own_sq[:, half * LANES:(half + 1) * LANES] = jnp.broadcast_to(squares(block), (LANES, LANES)).T[0:8]

    def fill(slot, half):
        block = feats[slot, half]
        g = lax.dot_general(block, own_rows[...], (((1,), (1,)), ((), ())), preferred_element_type=jnp.float32)
        e = (2.0 * g - squares(block) - own_sq[0:1, :]) * (1.0 / 128.0)
        at = pl.multiple_of((slot * 2 + half) * LANES, LANES)
        tile[pl.ds(at, LANES), :] = jnp.exp(e).astype(jnp.bfloat16)

    fill(me, 0)
    fill(me, 1)

    def direct(k, _):
        _, slot, _ = coset_peer(k)
        f_arrival(slot).wait_recv()
        g_copy(slot).start()
        fill(slot, c)
        return 0

    lax.fori_loop(1, CHIPS, direct, 0)

    def forwarded(k, _):
        _, slot, _ = coset_peer(k)
        g_arrival(slot).wait_recv()
        fill(slot, 1 - c)
        return 0

    lax.fori_loop(1, CHIPS, forwarded, 0)

    def first(k, _):
        _, slot, _ = coset_peer(k)

        @pl.when(k > 0)
        def _():
            t_copy(k, slot).wait_recv()

        for half in range(2):
            v = d_buf[slot, half]
            r_buf[slot, half] = v
            at = pl.multiple_of((slot * 2 + half) * LANES, LANES)
            w_buf[:, pl.ds(at, LANES)] = v.astype(jnp.bfloat16)
        return 0

    lax.fori_loop(0, CHIPS, first, 0)

    def q_copy(it, k, slot):
        peer, here, there = coset_peer(k)
        at = there if slot is None else slot
        return pltpu.make_async_remote_copy(
            q_buf.at[it, me], q_buf.at[it, at], q_send.at[it, k], q_recv.at[it, at],
            device_id=peer, device_id_type=MESH)

    def p_copy(it, k, slot):
        peer, _ = plane_peer(k)
        at = plane_me if slot is None else slot
        return pltpu.make_async_remote_copy(
            part.at[it, 0], plane.at[it, at], p_send.at[it, k], p_recv.at[it, at],
            device_id=peer, device_id_type=MESH)

    def z_copy(it, k, slot):
        peer, _ = line_peer(k)
        at = z if slot is None else slot
        return pltpu.make_async_remote_copy(
            part.at[it, 1], line.at[it, at], z_send.at[it, k], z_recv.at[it, at],
            device_id=peer, device_id_type=MESH)

    def exchange(it, stage, gathered, mine, copy, peer, pair):
        msg = jnp.concatenate(pair, axis=0)
        part[it, stage] = msg
        gathered[it, mine] = msg

        def send(k, _):
            copy(it, k, None).start()
            return 0

        lax.fori_loop(1, 16, send, 0)

    def collect(it, gathered, copy, peer):
        def wait(k, _):
            copy(it, k, peer(k)[1]).wait_recv()
            return 0

        lax.fori_loop(1, 16, wait, 0)
        return pair_tree((gathered[it, :, 0, :], gathered[it, :, 1, :]))

    for it in range(ITERS):
        own = jnp.dot(w_buf[:, :16 * LANES], tile[:16 * LANES], preferred_element_type=jnp.float32)
        others = jnp.dot(w_buf[:, 16 * LANES:], tile[16 * LANES:], preferred_element_type=jnp.float32)
        products = 2.0 * own + others
        slot_q = min(it, 1)
        sums = None
        fresh = []
        for half in range(2):
            d, r = d_buf[me, half], r_buf[me, half]
            q = d + products[:, half * LANES:(half + 1) * LANES]
            fresh.append(q)
            pairs = [two_prod(d, q), two_prod(r, q), two_prod(q, q), two_prod(r, r)]
            pair = tuple(jnp.concatenate([p[i] for p in pairs], axis=0) for i in range(2))
            sums = pair if sums is None else pair_add(sums, pair)
        if it < ITERS - 1:
            for half in range(2):
                q_buf[it, me, half] = fresh[half]
        pair = pair_tree(tuple(v.T for v in sums))
        exchange(it, 0, plane, plane_me, p_copy, plane_peer, pair)
        if it < ITERS - 1:
            def send_q(k, _):
                q_copy(it, k, None).start()
                return 0

            lax.fori_loop(1, CHIPS, send_q, 0)
        pair = collect(it, plane, p_copy, plane_peer)
        exchange(it, 1, line, z, z_copy, line_peer, pair)
        total = collect(it, line, z_copy, line_peer)

        def entry(i):
            return tuple(v[:, i * COLS:(i + 1) * COLS] for v in total)

        dq, rq, qq, rr = (entry(i) for i in range(4))
        step = rr[0] / dq[0]
        if it < ITERS - 1:
            zero = jnp.zeros_like(step)
            minus = pair_mul((-2.0 * step, zero), rq)
            plus = pair_mul(two_prod(step, step), qq)
            new = pair_add(pair_add(rr, minus), plus)
            ratio = new[0] / rr[0]
        else:
            ratio = jnp.zeros_like(step)
        scalars = jnp.concatenate([step, ratio, step, ratio], axis=1)
        scalars = jnp.broadcast_to(scalars, (LANES, LANES)).T
        s, beta = scalars[:COLS], scalars[COLS:2 * COLS]

        for half in range(2):
            gain = s * d_buf[me, half]
            out_ref[0, half] = gain if it == 0 else out_ref[0, half] + gain

        if it < ITERS - 1:
            def update(k, _):
                _, slot, _ = coset_peer(k)

                @pl.when(k > 0)
                def _():
                    q_copy(it, k, slot).wait_recv()

                for half in range(2):
                    r = r_buf[slot, half] - s * q_buf[it, slot, half]
                    d = r + beta * d_buf[slot, half]
                    r_buf[slot, half] = r
                    d_buf[slot, half] = d
                    at = pl.multiple_of((slot * 2 + half) * LANES, LANES)
                    w_buf[:, pl.ds(at, LANES)] = d.astype(jnp.bfloat16)
                return 0

            if it == 0:
                def sent(k, _):
                    t_copy(k, None).wait_send()
                    return 0

                lax.fori_loop(1, CHIPS, sent, 0)
            lax.fori_loop(0, CHIPS, update, 0)
        else:
            for half in range(2):
                out_ref[1, half] = r_buf[me, half] - s * fresh[half]


    def drain(k, _):
        f_copy(k).wait_send()
        _, slot, _ = coset_peer(k)
        g_copy(slot).wait_send()
        for it in range(ITERS - 1):
            q_copy(it, k, None).wait_send()
        return 0

    lax.fori_loop(1, CHIPS, drain, 0)

    def drain_sums(k, _):
        for it in range(ITERS):
            p_copy(it, k, None).wait_send()
            z_copy(it, k, None).wait_send()
        return 0

    lax.fori_loop(1, 16, drain_sums, 0)


def greet_all(barrier, peers):
    for peer in peers:
        pl.semaphore_signal(barrier, inc=1, device_id=peer, device_id_type=MESH)
    pl.semaphore_wait(barrier, len(peers))


def move_kernel(places, x_ref, t_ref, rows_ref, cols_ref, feats, cols, flipped, send, recv):
    blk, row = lax.axis_index("blk"), lax.axis_index("row")
    c = row % 2
    new_home = looked_up(places, blk)
    old_home = looked_up([places.index(b) for b in range(BLOCKS)], blk)
    homes = [(home, row - c + core) for home in (new_home, old_home) for core in range(2)]
    greet_all(pltpu.get_barrier_semaphore(), homes)

    def move(i, core, sender):
        return pltpu.make_async_remote_copy(
            (x_ref, flipped.at[core])[i], (feats, cols)[i].at[sender], send.at[i, core], recv.at[i, sender],
            device_id=homes[core], device_id_type=MESH)

    for core in range(2):
        move(0, core, c).start()
    turned = t_ref[...].T
    flipped[0] = turned[:COLS]
    flipped[1] = turned[COLS:]
    for core in range(2):
        move(1, core, c).start()
    for sender in range(2):
        move(0, 0, sender).wait_recv()
        move(1, 0, sender).wait_recv()
    rows_ref[...] = feats[...]
    cols_ref[...] = cols[...]
    for core in range(2):
        move(0, core, c).wait_send()
        move(1, core, c).wait_send()


def return_kernel(places, both_ref, sol_ref, res_ref, landed, send, recv):
    blk, row = lax.axis_index("blk"), lax.axis_index("row")
    c = row % 2
    new_home = looked_up(places, blk)
    old_home = looked_up([places.index(b) for b in range(BLOCKS)], blk)
    homes = [(home, row - c + core) for home in (old_home, new_home) for core in range(2)]
    greet_all(pltpu.get_barrier_semaphore(), homes)

    def move(i, core, sender):
        return pltpu.make_async_remote_copy(
            both_ref.at[i, core], landed.at[i, sender], send.at[i, core], recv.at[i, sender],
            device_id=homes[core], device_id_type=MESH)

    for i in range(2):
        for core in range(2):
            move(i, core, c).start()
    for i, out in ((0, sol_ref), (1, res_ref)):
        for sender in range(2):
            move(i, 0, sender).wait_recv()
        out[...] = jnp.concatenate([landed[i, 0], landed[i, 1]], axis=0).T
    for i in range(2):
        for core in range(2):
            move(i, core, c).wait_send()


def call(body, ident, outs, scratch, *args):
    vmem = pl.BlockSpec(memory_space=pltpu.VMEM)
    return pl.pallas_call(
        body,
        out_shape=[jax.ShapeDtypeStruct(shape, kind) for shape, kind in outs],
        in_specs=[vmem] * len(args),
        out_specs=[vmem] * len(outs),
        scratch_shapes=scratch,
        compiler_params=pltpu.CompilerParams(
            collective_id=ident, has_side_effects=True, vmem_limit_bytes=40 * 1024 * 1024
        ),
    )(*args)


def moved(mask, features, targets):
    dma = pltpu.SemaphoreType.DMA
    rows, cols = ((2, LANES, LANES), jnp.bfloat16), ((2, COLS, LANES), jnp.float32)
    return tuple(call(
        functools.partial(move_kernel, placement(mask)), mask, [rows, cols],
        [pltpu.VMEM(*rows), pltpu.VMEM(*cols), pltpu.VMEM(*cols), dma((2, 2)), dma((2, 2))], features, targets))


def returned(mask, both):
    dma = pltpu.SemaphoreType.DMA
    out = ((LANES, 2 * COLS), jnp.float32)
    return tuple(call(
        functools.partial(return_kernel, placement(mask)), LAST + mask, [out, out],
        [pltpu.VMEM(both.shape, jnp.float32), dma((2, 2)), dma((2, 2))], both))


def conjugate_gradients(features, targets):
    f32, bf16 = jnp.float32, jnp.bfloat16
    dma = pltpu.SemaphoreType.DMA
    chips = dma((CHIPS,))
    sums = dma((ITERS, 16))
    scratch = [
        pltpu.VMEM((CHIPS, 2, LANES, LANES), bf16),
        pltpu.VMEM((CHIPS * 2 * LANES, 2 * LANES), bf16),
        pltpu.VMEM((2, CHIPS, 2, COLS, LANES), f32),
        pltpu.VMEM((CHIPS, 2, COLS, LANES), f32),
        pltpu.VMEM((CHIPS, 2, COLS, LANES), f32),
        pltpu.VMEM((COLS, CHIPS * 2 * LANES), bf16),
        pltpu.VMEM((ITERS, 2, 2, LANES), f32),
        pltpu.VMEM((ITERS, 16, 2, LANES), f32),
        pltpu.VMEM((ITERS, 16, 2, LANES), f32),
        pltpu.VMEM((2 * LANES, LANES), bf16),
        pltpu.VMEM((8, 2 * LANES), f32),
        chips, chips, chips, chips, chips, chips, dma((2, CHIPS)), dma((2, CHIPS)), sums, sums, sums, sums,
    ]
    return call(kernel, 0, [((2, 2, COLS, LANES), f32)], scratch, features, targets)[0]


def local(features, targets, round_masks):
    which = jnp.clip(round_masks[0] + round_masks[1] - LAST - 1, 0, LAST - 2)
    masks = range(1, LAST)
    features, targets = lax.switch(which, [functools.partial(moved, m) for m in masks], features, targets)
    both = conjugate_gradients(features, targets)
    return lax.switch(which, [functools.partial(returned, m) for m in masks], both)


def solution(mesh):
    in_specs = (P(("blk", "row"), None), P(("blk", "row"), None), P())
    out_specs = (P(("blk", "row"), None), P(("blk", "row"), None))
    return jax.shard_map(local, mesh=mesh, in_specs=in_specs, out_specs=out_specs, check_vma=False)
```

```python
import functools

import jax
import jax.numpy as jnp
import numpy as np
from jax import lax
from jax.experimental import pallas as pl
from jax.experimental.pallas import tpu as pltpu
from jax.sharding import PartitionSpec as P

MESH = pl.DeviceIdType.MESH
ITERS = 3
BLOCKS = 32
LAST = BLOCKS - 1
NEAR, ACROSS = 1, 16
NX, NYL, NZ = 4, 2, 16
CHIPS = 3 * NX * NYL
COLS = 32
LANES = 128


def hops(a, b):
    dz = abs(a % NZ - b % NZ)
    return min(dz, NZ - dz) + 2 * (a // NZ != b // NZ)


def placement(mask):
    groups, seen = [], set()
    for b in range(BLOCKS):
        if b not in seen:
            group = [b, b ^ LAST, b ^ mask, b ^ LAST ^ mask]
            seen.update(group)
            groups.append(group)
    offsets = [0, NEAR, ACROSS, NEAR ^ ACROSS]

    def cost(group, base, twist):
        lengths = [hops(b, base ^ o ^ twist) for b, o in zip(group, offsets)]
        return (max(lengths) if min(lengths) else BLOCKS), sum(lengths)

    bases = [p for p in range(BLOCKS) if not p & (NEAR | ACROSS)]
    best = [[min((cost(g, base, t), t) for t in offsets) for base in bases] for g in groups]
    state = {0: ((0, 0), [])}
    for g in range(len(groups)):
        following = {}
        for used, ((longest, total), chosen) in state.items():
            for i in range(len(bases)):
                if used >> i & 1:
                    continue
                (top, plus), twist = best[g][i]
                value = (max(longest, top), total + plus)
                key = used | 1 << i
                if key not in following or value < following[key][0]:
                    following[key] = (value, chosen + [(i, twist)])
        state = following
    _, chosen = state[(1 << len(bases)) - 1]
    place = [0] * BLOCKS
    for group, (i, twist) in zip(groups, chosen):
        for b, o in zip(group, offsets):
            place[b] = bases[i] ^ o ^ twist
    return place


def two_sum(a, b):
    s = a + b
    bb = s - a
    return s, (a - (s - bb)) + (b - bb)


def renorm(s, e):
    h = s + e
    return h, e - (h - s)


def pair_add(a, b):
    s, e = two_sum(a[0], b[0])
    return renorm(s, e + (a[1] + b[1]))


def split(a):
    c = 4097.0 * a
    h = c - (c - a)
    return h, a - h


def two_prod(a, b):
    p = a * b
    ah, al = split(a)
    bh, bl = split(b)
    return p, ((ah * bh - p) + ah * bl + al * bh) + al * bl


def pair_mul(a, b):
    p, e = two_prod(a[0], b[0])
    return renorm(p, e + (a[0] * b[1] + a[1] * b[0]))


def pair_tree(pair):
    n = pair[0].shape[0]
    while n > 1:
        n //= 2
        pair = pair_add(tuple(v[:n] for v in pair), tuple(v[n:] for v in pair))
    return pair


def squares(block):
    wide = block.astype(jnp.float32)
    return jnp.sum(wide * wide, axis=1, keepdims=True)


def looked_up(table, index):
    value = jnp.int32(table[0])
    for i in range(1, len(table)):
        value = jnp.where(index == i, table[i], value)
    return value


def kernel(
    x_ref, t_ref, out_ref,
    feats, tile, q_buf, r_buf, d_buf, w_buf, part, plane, line, own_rows, own_sq,
    f_send, f_recv, g_send, g_recv, t_send, t_recv, q_send, q_recv, p_send, p_recv, z_send, z_recv,
):
    blk, row = lax.axis_index("blk"), lax.axis_index("row")
    yh, z = blk // NZ, blk % NZ
    x, yl, c = row // 4, (row // 2) % 2, row % 2
    chip = x * NYL + yl
    me = chip

    def slot_of(px, u):
        return (u // 2) * 8 + px * NYL + u % 2

    def column(v):
        return (v // 2) * 2 + (yl + v) % 2

    def direct_peer(k):
        v, dx = k % 6, k // 6 + k // 12
        side, pyl = v // 2, (yl + v) % 2
        near = jnp.where(side == 1, 1, 0)
        across = jnp.where(side == 2, 1, 0)
        pz = z + near * (1 - 2 * (z % 2))
        pyh = (yh + across) % 2
        return (pyh * NZ + pz, ((x + dx) % NX) * 4 + pyl * 2 + c), slot_of(x, side * 2 + yl)

    def near_peer(k):
        return direct_peer(6 * (k // 2) + 2 + k % 2)

    def beside_peer(way):
        return (blk, ((x + 1 + 2 * way) % NX) * 4 + yl * 2 + c)

    def spread(view, send, recv):
        def copy(ref, there, s, r, peer):
            return pltpu.make_async_remote_copy(
                ref, there, send.at[s], recv.at[r], device_id=peer, device_id_type=MESH)

        def direct(k):
            peer, there = direct_peer(k)
            return copy(view(me), view(there), k, there, peer)

        def beyond(u, way):
            slot = slot_of((x + 3 + 2 * way) % NX, u)
            part = view(slot, way)
            return copy(part, part, 18 + 2 * u + way, CHIPS + u if way else slot, beside_peer(way))

        def arrived(slot):
            copy(view(slot), view(slot), 0, slot, (blk, row)).wait_recv()

        def arrived_far(u):
            slot = slot_of((x + 2) % NX, u)
            for way in range(2):
                part = view(slot, way)
                copy(part, part, 0, CHIPS + u if way else slot, (blk, row)).wait_recv()
            return slot

        def start():
            for first, last in ((6, 18), (1, 6)):
                lax.fori_loop(first, last, lambda k, _: direct(k).start() or 0, 0)

        def second(v):
            slot = slot_of(x, column(v))
            arrived(slot)
            return slot

        def third(u, way):
            slot = slot_of((x + 3 + 2 * way) % NX, u)
            arrived(slot)
            beyond(u, way).start()
            return slot

        def drain():
            lax.fori_loop(1, 18, lambda k, _: direct(k).wait_send() or 0, 0)
            for way in range(2):
                lax.fori_loop(0, 6, lambda u, _, way=way: beyond(u, way).wait_send() or 0, 0)

        return start, second, third, arrived_far, drain

    def plane_peer(k):
        y = (yh * 2 + yl + k) % 4
        px = (x + k // 4) % NX
        return ((y // 2) * NZ + z, px * 4 + (y % 2) * 2 + c), px * 4 + y

    def line_peer(k):
        pz = (z + k) % NZ
        return (yh * NZ + pz, row), pz

    plane_me = x * 4 + yh * 2 + yl

    barrier = pltpu.get_barrier_semaphore()

    def greet(peer):
        pl.semaphore_signal(barrier, inc=1, device_id=peer, device_id_type=MESH)

    greet((blk, row - c + (1 - c)))
    for first, last, peer in ((0, 6, near_peer), (1, 16, plane_peer), (1, 16, line_peer)):
        lax.fori_loop(first, last, lambda k, _, peer=peer: greet(peer(k)[0]) or 0, 0)

    def g_copy(slot):
        return pltpu.make_async_remote_copy(
            feats.at[slot, c], feats.at[slot, c], g_send.at[slot], g_recv.at[slot],
            device_id=(blk, row - c + (1 - c)), device_id_type=MESH)

    def g_arrival(slot):
        return pltpu.make_async_remote_copy(
            feats.at[slot, 1 - c], feats.at[slot, 1 - c], g_send.at[slot], g_recv.at[slot],
            device_id=(blk, row - c + (1 - c)), device_id_type=MESH)

    def f_view(slot, way=None):
        return feats.at[slot, c] if way is None else feats.at[slot, c, pl.ds(way * (LANES // 2), LANES // 2)]

    def t_view(slot, way=None):
        return d_buf.at[slot] if way is None else d_buf.at[slot, way]

    def q_view(it, slot, way=None):
        return q_buf.at[it, slot] if way is None else q_buf.at[it, slot, way]

    f_start, f_second, f_third, f_far, f_drain = spread(f_view, f_send, f_recv)
    t_start, t_second, t_third, t_far, t_drain = spread(t_view, t_send, t_recv)
    for half in range(2):
        block = x_ref[half]
        feats[me, half] = block
        own_rows[half * LANES:(half + 1) * LANES] = block
        own_sq[:, half * LANES:(half + 1) * LANES] = jnp.broadcast_to(squares(block), (LANES, LANES)).T[0:8]

    def fill(slot, half):
        block = feats[slot, half]
        g = lax.dot_general(block, own_rows[...], (((1,), (1,)), ((), ())), preferred_element_type=jnp.float32)
        e = (2.0 * g - squares(block) - own_sq[0:1, :]) * (1.0 / 128.0)
        at = pl.multiple_of((slot * 2 + half) * LANES, LANES)
        tile[pl.ds(at, LANES), :] = jnp.exp(e).astype(jnp.bfloat16)

    fill(me, 0)
    fill(me, 1)
    d_buf[me] = t_ref[...]

    pl.semaphore_wait(barrier, 1 + 6 + 15 + 15)
    f_start()
    t_start()

    def loop(first, last, body):
        def step(i, carry):
            body(i)
            return carry

        lax.fori_loop(first, last, step, 0)

    def pass_on(slot):
        g_copy(slot).start()

    def second_all(v):
        pass_on(f_second(v))

    def third_all(u):
        for way in range(2):
            pass_on(f_third(u, way))

    def far_all(u):
        pass_on(f_far(u))

    loop(0, 6, third_all)
    loop(1, 6, second_all)
    loop(1, 6, lambda v: fill(slot_of(x, column(v)), c))

    def fill_beside(u):
        fill(slot_of((x + 1) % NX, u), c)
        fill(slot_of((x + 3) % NX, u), c)

    loop(0, 6, fill_beside)
    loop(0, 6, far_all)
    for way in range(2):
        loop(0, 6, lambda u, way=way: t_third(u, way))
    loop(0, 6, lambda u: fill(slot_of((x + 2) % NX, u), c))

    def forwarded(slot):
        g_arrival(slot).wait_recv()
        fill(slot, 1 - c)

    loop(1, 6, lambda v: forwarded(slot_of(x, column(v))))
    for dx in (1, 3, 2):
        loop(0, 6, lambda u, dx=dx: forwarded(slot_of((x + dx) % NX, u)))
    loop(1, 6, t_second)
    loop(0, 6, t_far)

    def first(slot):
        for half in range(2):
            v = d_buf[slot, half]
            r_buf[slot, half] = v
            at = pl.multiple_of((slot * 2 + half) * LANES, LANES)
            w_buf[:, pl.ds(at, LANES)] = v.astype(jnp.bfloat16)

    loop(0, CHIPS, first)

    def p_copy(it, k, slot):
        peer, _ = plane_peer(k)
        at = plane_me if slot is None else slot
        return pltpu.make_async_remote_copy(
            part.at[it, 0], plane.at[it, at], p_send.at[it, k], p_recv.at[it, at],
            device_id=peer, device_id_type=MESH)

    def z_copy(it, k, slot):
        peer, _ = line_peer(k)
        at = z if slot is None else slot
        return pltpu.make_async_remote_copy(
            part.at[it, 1], line.at[it, at], z_send.at[it, k], z_recv.at[it, at],
            device_id=peer, device_id_type=MESH)

    def exchange(it, stage, gathered, mine, copy, peer, pair):
        msg = jnp.concatenate(pair, axis=0)
        part[it, stage] = msg
        gathered[it, mine] = msg

        def send(i, _):
            k = 8 + (i // 2) * (1 - 2 * (i % 2))
            copy(it, k, None).start()
            return 0

        lax.fori_loop(1, 16, send, 0)

    def collect(it, gathered, copy, peer):
        def wait(k, _):
            copy(it, k, peer(k)[1]).wait_recv()
            return 0

        lax.fori_loop(1, 16, wait, 0)
        return pair_tree((gathered[it, :, 0, :], gathered[it, :, 1, :]))

    q_drains = []
    for it in range(ITERS):
        own = jnp.dot(w_buf[:, :16 * LANES], tile[:16 * LANES], preferred_element_type=jnp.float32)
        others = jnp.dot(w_buf[:, 16 * LANES:], tile[16 * LANES:], preferred_element_type=jnp.float32)
        products = 2.0 * own + others
        slot_q = min(it, 1)
        sums = None
        fresh = []
        for half in range(2):
            d, r = d_buf[me, half], r_buf[me, half]
            q = d + products[:, half * LANES:(half + 1) * LANES]
            fresh.append(q)
            pairs = [two_prod(d, q), two_prod(r, q), two_prod(q, q), two_prod(r, r)]
            pair = tuple(jnp.concatenate([p[i] for p in pairs], axis=0) for i in range(2))
            sums = pair if sums is None else pair_add(sums, pair)
        if it < ITERS - 1:
            for half in range(2):
                q_buf[it, me, half] = fresh[half]
        pair = pair_tree(tuple(v.T for v in sums))
        exchange(it, 0, plane, plane_me, p_copy, plane_peer, pair)
        if it < ITERS - 1:
            q_start, q_second, q_third, q_far, q_drain = spread(
                functools.partial(q_view, it), q_send.at[it], q_recv.at[it])
            q_drains.append(q_drain)
            q_start()
        pair = collect(it, plane, p_copy, plane_peer)
        exchange(it, 1, line, z, z_copy, line_peer, pair)
        if it < ITERS - 1:
            loop(0, 6, lambda u: [q_third(u, way) for way in range(2)])
            loop(1, 6, q_second)
            loop(0, 6, q_far)
        total = collect(it, line, z_copy, line_peer)

        def entry(i):
            return tuple(v[:, i * COLS:(i + 1) * COLS] for v in total)

        dq, rq, qq, rr = (entry(i) for i in range(4))
        step = rr[0] / dq[0]
        if it < ITERS - 1:
            zero = jnp.zeros_like(step)
            minus = pair_mul((-2.0 * step, zero), rq)
            plus = pair_mul(two_prod(step, step), qq)
            new = pair_add(pair_add(rr, minus), plus)
            ratio = new[0] / rr[0]
        else:
            ratio = jnp.zeros_like(step)
        scalars = jnp.concatenate([step, ratio, step, ratio], axis=1)
        scalars = jnp.broadcast_to(scalars, (LANES, LANES)).T
        s, beta = scalars[:COLS], scalars[COLS:2 * COLS]

        for half in range(2):
            gain = s * d_buf[me, half]
            out_ref[0, half] = gain if it == 0 else out_ref[0, half] + gain

        if it < ITERS - 1:
            def update(slot):
                for half in range(2):
                    r = r_buf[slot, half] - s * q_buf[it, slot, half]
                    d = r + beta * d_buf[slot, half]
                    r_buf[slot, half] = r
                    d_buf[slot, half] = d
                    at = pl.multiple_of((slot * 2 + half) * LANES, LANES)
                    w_buf[:, pl.ds(at, LANES)] = d.astype(jnp.bfloat16)

            if it == 0:
                t_drain()
            loop(0, CHIPS, update)
        else:
            for half in range(2):
                out_ref[1, half] = r_buf[me, half] - s * fresh[half]


    f_drain()
    for q_drain in q_drains:
        q_drain()
    loop(1, 6, lambda v: g_copy(slot_of(x, column(v))).wait_send())
    for dx in range(1, NX):
        loop(0, 6, lambda u, dx=dx: g_copy(slot_of((x + dx) % NX, u)).wait_send())

    def drain_sums(k, _):
        for it in range(ITERS):
            p_copy(it, k, None).wait_send()
            z_copy(it, k, None).wait_send()
        return 0

    lax.fori_loop(1, 16, drain_sums, 0)


def greet_all(barrier, peers):
    for peer in peers:
        pl.semaphore_signal(barrier, inc=1, device_id=peer, device_id_type=MESH)


def move_kernel(places, x_ref, t_ref, rows_ref, cols_ref, feats, cols, flipped, send, recv):
    blk, row = lax.axis_index("blk"), lax.axis_index("row")
    c = row % 2
    new_home = looked_up(places, blk)
    old_home = looked_up([places.index(b) for b in range(BLOCKS)], blk)
    homes = [(home, row - c + core) for home in (new_home, old_home) for core in range(2)]
    barrier = pltpu.get_barrier_semaphore()
    greet_all(barrier, homes)
    turned = t_ref[...].T
    flipped[0] = turned[:COLS]
    flipped[1] = turned[COLS:]
    pl.semaphore_wait(barrier, len(homes))

    def move(i, core, sender):
        return pltpu.make_async_remote_copy(
            (x_ref, flipped.at[core])[i], (feats, cols)[i].at[sender], send.at[i, core], recv.at[i, sender],
            device_id=homes[core], device_id_type=MESH)

    for i in range(2):
        for core in range(2):
            move(i, core, c).start()
    for sender in range(2):
        move(0, 0, sender).wait_recv()
        move(1, 0, sender).wait_recv()
    rows_ref[...] = feats[...]
    cols_ref[...] = cols[...]
    for core in range(2):
        move(0, core, c).wait_send()
        move(1, core, c).wait_send()


def return_kernel(places, both_ref, sol_ref, res_ref, landed, send, recv):
    blk, row = lax.axis_index("blk"), lax.axis_index("row")
    c = row % 2
    new_home = looked_up(places, blk)
    old_home = looked_up([places.index(b) for b in range(BLOCKS)], blk)
    homes = [(home, row - c + core) for home in (old_home, new_home) for core in range(2)]
    barrier = pltpu.get_barrier_semaphore()
    greet_all(barrier, homes)
    pl.semaphore_wait(barrier, len(homes))

    def move(i, core, sender):
        return pltpu.make_async_remote_copy(
            both_ref.at[i, core], landed.at[i, sender], send.at[i, core], recv.at[i, sender],
            device_id=homes[core], device_id_type=MESH)

    for i in range(2):
        for core in range(2):
            move(i, core, c).start()
    for i, out in ((0, sol_ref), (1, res_ref)):
        for sender in range(2):
            move(i, 0, sender).wait_recv()
        out[...] = jnp.concatenate([landed[i, 0], landed[i, 1]], axis=0).T
    for i in range(2):
        for core in range(2):
            move(i, core, c).wait_send()


def call(body, ident, outs, scratch, *args):
    vmem = pl.BlockSpec(memory_space=pltpu.VMEM)
    return pl.pallas_call(
        body,
        out_shape=[jax.ShapeDtypeStruct(shape, kind) for shape, kind in outs],
        in_specs=[vmem] * len(args),
        out_specs=[vmem] * len(outs),
        scratch_shapes=scratch,
        compiler_params=pltpu.CompilerParams(
            collective_id=ident, has_side_effects=True, vmem_limit_bytes=40 * 1024 * 1024
        ),
    )(*args)


def moved(mask, features, targets):
    dma = pltpu.SemaphoreType.DMA
    rows, cols = ((2, LANES, LANES), jnp.bfloat16), ((2, COLS, LANES), jnp.float32)
    return tuple(call(
        functools.partial(move_kernel, placement(mask)), mask, [rows, cols],
        [pltpu.VMEM(*rows), pltpu.VMEM(*cols), pltpu.VMEM(*cols), dma((2, 2)), dma((2, 2))], features, targets))


def returned(mask, both):
    dma = pltpu.SemaphoreType.DMA
    out = ((LANES, 2 * COLS), jnp.float32)
    return tuple(call(
        functools.partial(return_kernel, placement(mask)), LAST + mask, [out, out],
        [pltpu.VMEM(both.shape, jnp.float32), dma((2, 2)), dma((2, 2))], both))


def conjugate_gradients(features, targets):
    f32, bf16 = jnp.float32, jnp.bfloat16
    dma = pltpu.SemaphoreType.DMA
    chips, ways = dma((CHIPS,)), dma((CHIPS + 6,))
    sums = dma((ITERS, 16))
    scratch = [
        pltpu.VMEM((CHIPS, 2, LANES, LANES), bf16),
        pltpu.VMEM((CHIPS * 2 * LANES, 2 * LANES), bf16),
        pltpu.VMEM((2, CHIPS, 2, COLS, LANES), f32),
        pltpu.VMEM((CHIPS, 2, COLS, LANES), f32),
        pltpu.VMEM((CHIPS, 2, COLS, LANES), f32),
        pltpu.VMEM((COLS, CHIPS * 2 * LANES), bf16),
        pltpu.VMEM((ITERS, 2, 2, LANES), f32),
        pltpu.VMEM((ITERS, 16, 2, LANES), f32),
        pltpu.VMEM((ITERS, 16, 2, LANES), f32),
        pltpu.VMEM((2 * LANES, LANES), bf16),
        pltpu.VMEM((8, 2 * LANES), f32),
        ways, ways, chips, chips, ways, ways, dma((2, CHIPS + 6)), dma((2, CHIPS + 6)), sums, sums, sums, sums,
    ]
    return call(kernel, 0, [((2, 2, COLS, LANES), f32)], scratch, features, targets)[0]


def local(features, targets, round_masks):
    which = jnp.clip(round_masks[0] + round_masks[1] - LAST - 1, 0, LAST - 2)
    masks = range(1, LAST)
    features, targets = lax.switch(which, [functools.partial(moved, m) for m in masks], features, targets)
    both = conjugate_gradients(features, targets)
    return lax.switch(which, [functools.partial(returned, m) for m in masks], both)


def solution(mesh):
    in_specs = (P(("blk", "row"), None), P(("blk", "row"), None), P())
    out_specs = (P(("blk", "row"), None), P(("blk", "row"), None))
    return jax.shard_map(local, mesh=mesh, in_specs=in_specs, out_specs=out_specs, check_vma=False)
```
